256 devices in a mesh: dp: 4 (over y), seq: 64 (over x, z, core).
Axes of the slice: x: 4, y: 4, z: 8, core: 2. Of those that a mesh axis runs over, the one named last changes fastest.
Arguments:
- values: bfloat16 [8, 49152, 1024], P('dp', 'seq'), may hold values from -6 to 6
- gates: bfloat16 [8, 49152, 1024], P('dp', 'seq'), may hold values from 0.25 to 4
- grad_out: bfloat16 [8, 49152, 1024], P('dp', 'seq'), may hold values from -4 to 4
- first_blocks: bfloat16 [192, 256, 256], P('seq'), may hold values from -0.375 to 0.375
- second_blocks: bfloat16 [256, 192, 192], P('seq'), may hold values from -0.4375 to 0.4375
Outputs:
- grad_values: bfloat16 [8, 49152, 1024], P('dp', 'seq')
- grad_first: float32 [192, 256, 256], P('seq')
- grad_second: float32 [256, 192, 192], P('seq')
The draws below stay inside these ranges and needn't reach their ends.
All inputs are finite; a program needn't handle non-finite values.
Results may differ from the reference program's by a relative error of at most 0.0058.
Values may be sent and summed in bfloat16 or wider, within the bound.
No kernel may reach another device: no remote copies, remote signals or barrier semaphores. Data moves between devices by JAX's collectives and lax.ppermute only.
A program may use at most 128 MiB of HBM per device.

```python
import math
import jax
import jax.numpy as jnp
from jax import lax

A = 192
B = 256
D = 1024
BATCH = 8
L = 49152


def block_levels(rng, extent, split, low, high):
    loudness = 1.0
    for position, parts in split:
        draws = jax.random.uniform(jax.random.fold_in(jax.random.fold_in(rng, 6), position), (parts,), jnp.float32, low / len(split), high / len(split))
        loudness = loudness * jnp.repeat(jnp.exp(draws), extent[position] // parts).reshape((-1,) + (1,) * (len(extent) - 1 - position))
    return loudness


def scatter_about(stream_key, shape, width, limit, split=(), held_as=jnp.bfloat16):
    array = jax.random.normal(stream_key, shape, jnp.float32) * width
    if len(split) > 0:
        array = block_levels(stream_key, shape, split, -0.22, 0.18) * array
    return jnp.clip(array, min=-limit, max=limit).astype(held_as)


def setup_inputs(seed: int = 0) -> dict:
    streams_of = jax.random.split(jax.random.key(seed), 6)
    values = scatter_about(streams_of[0], (BATCH, L, D), 1.0, 6.0, ((0, 4), (1, 64)))
    gates = jnp.clip(jnp.exp(math.log(4.0) - 2.7725887 * jax.random.uniform(streams_of[1], (BATCH, L, D), jnp.float32) ** block_levels(streams_of[1], (BATCH, L, D), ((0, 4), (1, 64)), -0.2, 0.2)), 0.25, 4.0).astype(jnp.bfloat16)
    grad_out = scatter_about(streams_of[2], (BATCH, L, D), 0.25, 4.0, ((0, 4), (1, 64)))
    first_blocks = scatter_about(streams_of[3], (A, B, B), B ** -0.5, 0.375, ((0, 64),))
    second_blocks = scatter_about(streams_of[4], (B, A, A), A ** -0.5, 0.4375, ((0, 64),))
    return {"values": values, "gates": gates, "grad_out": grad_out, "first_blocks": first_blocks, "second_blocks": second_blocks}


def reference(values, gates, grad_out, first_blocks, second_blocks):
    first_wide = first_blocks.astype(jnp.float32)
    second_wide = second_blocks.astype(jnp.float32)

    def step(carry, inputs):
        acc_first, acc_second = carry
        seq_values, seq_gates, seq_grad = inputs
        inputs_wide = seq_values.reshape(A, B, D).astype(jnp.float32)
        mixed = jnp.einsum('abd,abc->acd', inputs_wide, first_wide).astype(jnp.bfloat16)
        scaled = (seq_grad.astype(jnp.float32) * seq_gates.astype(jnp.float32)).astype(jnp.bfloat16)
        scaled_wide = scaled.reshape(A, B, D).astype(jnp.float32)
        mixed_wide = mixed.astype(jnp.float32)
        acc_second = acc_second + jnp.einsum('acd,ecd->cae', mixed_wide, scaled_wide)
        inner = jnp.einsum('cae,ecd->acd', second_wide, scaled_wide).astype(jnp.bfloat16)
        inner_wide = inner.astype(jnp.float32)
        acc_first = acc_first + jnp.einsum('abd,acd->abc', inputs_wide, inner_wide)
        result = jnp.einsum('abc,acd->abd', first_wide, inner_wide).astype(jnp.bfloat16)
        return (acc_first, acc_second), result.reshape(A * B, D)

    start = (jnp.zeros((A, B, B), jnp.float32), jnp.zeros((B, A, A), jnp.float32))
    (grad_first, grad_second), grad_values = lax.scan(step, start, (values, gates, grad_out))
    return grad_values, grad_first, grad_second
```

```python
import jax
import jax.numpy as jnp
from jax import lax
from jax.sharding import PartitionSpec as P

X, Z, C = 4, 8, 2
F32, BF16 = jnp.float32, jnp.bfloat16


def spot(x, z, c):
    return ((x % X) * Z + z % Z) * C + c % C


def moved(dx, dz, dc):
    return [
        (spot(x, z, c), spot(x + dx, z + dz, c + dc))
        for x in range(X)
        for z in range(Z)
        for c in range(C)
    ]


ROWS = [[spot(x, z, c) for x in range(X)] for z in range(Z) for c in range(C)]
STEPS = (4, 1, 7, 2, 6, 3, 5)


def hop(array, dz):
    return lax.ppermute(array, "seq", moved(0, dz, 0))


def swap(array):
    return lax.ppermute(array, "seq", moved(0, 0, 1))


def across(array):
    return lax.all_to_all(array, "seq", 0, 0, axis_index_groups=ROWS, tiled=True)


def after(array, earlier):
    return lax.optimization_barrier((array, earlier))[0]


def along(pieces, earlier):
    got = [pieces[0]] + [None] * (Z - 1)
    for k in STEPS:
        piece = pieces[k] if earlier is None else after(pieces[k], earlier[k])
        got[k] = hop(piece, k)
    return got


def dp_sum(array):
    n = 4
    me = lax.axis_index("dp")
    parts = array.reshape((n, -1) + array.shape[1:])
    total = lax.dynamic_index_in_dim(parts, me, 0, keepdims=False)
    for k in range(1, n):
        part = lax.dynamic_index_in_dim(parts, (me + k) % n, 0, keepdims=False).astype(BF16)
        total += lax.ppermute(part, "dp", [(i, (i + k) % n) for i in range(n)]).astype(F32)
    out = jnp.zeros_like(parts)
    out = lax.dynamic_update_index_in_dim(out, total, me, 0)
    sent = total.astype(BF16)
    for k in range(1, n):
        part = lax.ppermute(sent, "dp", [(i, (i + k) % n) for i in range(n)]).astype(F32)
        out = lax.dynamic_update_index_in_dim(out, part, (me - k) % n, 0)
    return out.reshape(array.shape)


def shards(values, gates, grad_out, first_blocks, second_blocks):
    count, rows, width = values.shape
    A3, B = first_blocks.shape[:2]
    C8 = B // (X * Z)
    C4, A = second_blocks.shape[:2]
    here = lax.axis_index("seq")
    core, z = here % C, (here // C) % Z
    up = (z + jnp.arange(Z)) % Z
    down = (z - jnp.arange(Z)) % Z

    view = (A3, X, Z, C8, width)
    moved_g, earlier = [], None
    for n in range(count):
        a, b = gates[n].reshape(view), grad_out[n].reshape(view)
        pieces = []
        for k in range(Z):
            at = (z + k) % Z
            p = lax.dynamic_index_in_dim(a, at, 2, keepdims=False).astype(F32)
            q = lax.dynamic_index_in_dim(b, at, 2, keepdims=False).astype(F32)
            pieces.append((p * q).astype(BF16))
        earlier = along(pieces, earlier)
        moved_g.append(earlier)

    first = first_blocks.reshape(A3, B, X, Z, C8)
    first_up = jnp.take(first, up, axis=3).reshape(A3, B, B)
    inputs = values.reshape(count, A3, B, width)
    across_u = []
    for n in range(count):
        mixed = jnp.einsum("abd,abc->acd", inputs[n], first_up, preferred_element_type=F32)
        mixed = mixed.astype(BF16).reshape(A3, X, Z, C8, width)
        across_u.append(across(mixed.transpose(1, 0, 2, 3, 4)))

    second = second_blocks.reshape(C4, A // (C * A3), C, A3, A)
    mine = lax.dynamic_index_in_dim(second, core, 2, keepdims=False)
    other = swap(lax.dynamic_index_in_dim(second, 1 - core, 2, keepdims=False))
    pair = jnp.where(core == 0, jnp.stack([mine, other]), jnp.stack([other, mine]))
    pair = pair.reshape(C8, X, Z, A3, X, Z, C, A3)
    pair = jnp.take(jnp.take(pair, up, axis=2), down, axis=5)
    pair = jnp.where(core == 0, pair, pair[:, :, :, :, :, :, ::-1])
    pair = pair.transpose(0, 1, 2, 3, 6, 4, 5, 7).reshape(C8, A // C, C, A // C)

    cols_g = []
    for n in range(count):
        own = across(jnp.stack(moved_g[n]).transpose(2, 0, 1, 3, 4))
        own = own.reshape(A // C, C8, width)
        cols_g.append(jnp.stack([own, swap(own)]))

    moved_u = []
    for n in range(count):
        part = across_u[n].reshape(X, A3, Z, C8, width)
        earlier = along([part[:, :, k] for k in range(Z)], earlier)
        moved_u.append(earlier)

    across_v = []
    for n in range(count):
        inner = jnp.einsum("came,mecd->acd", pair, cols_g[n], preferred_element_type=F32)
        across_v.append(across(inner.astype(BF16).reshape(X, Z, A3, C8, width)))

    moved_v = []
    for n in range(count):
        earlier = along([across_v[n][:, k] for k in range(Z)], earlier)
        moved_v.append(earlier)

    grad_second = 0
    for n in range(count):
        cols_u = jnp.stack(moved_u[n]).reshape(A // C, C8, width)
        grad_second += jnp.einsum("acd,mecd->came", cols_u, cols_g[n], preferred_element_type=F32)
    grad_second = grad_second.reshape(C, C4, A // C, C, A // C)
    mine = lax.dynamic_index_in_dim(grad_second, core, 0, keepdims=False)
    other = swap(lax.dynamic_index_in_dim(grad_second, 1 - core, 0, keepdims=False))
    other = other[:, :, ::-1]
    pair = jnp.where(core == 0, jnp.stack([mine, other]), jnp.stack([other, mine]))
    pair = jnp.where(core == 0, pair, pair[:, :, :, ::-1])
    pair = pair.reshape(C, C4, Z, X, A3, C, X, Z, A3)
    pair = jnp.take(jnp.take(pair, down, axis=2), down, axis=7)
    pair = pair.transpose(1, 3, 2, 0, 4, 6, 7, 5, 8).reshape(C4, A, A)
    grad_second = lax.psum(pair, "dp")

    grad_first = 0
    results = []
    for n in range(count):
        inner = jnp.zeros((A3, X, Z, C8, width), BF16)
        for k in range(Z):
            piece = moved_v[n][k].transpose(1, 0, 2, 3)
            inner = lax.dynamic_update_index_in_dim(inner, piece, (z - k) % Z, 2)
        inner = inner.reshape(A3, B, width)
        grad_first += jnp.einsum("abd,acd->abc", inputs[n], inner, preferred_element_type=F32)
        results.append(
            jnp.einsum("abc,acd->abd", first_blocks, inner, preferred_element_type=F32).astype(BF16)
        )
    grad_values = jnp.stack(results).reshape(count, rows, width)
    grad_first = dp_sum(grad_first.reshape(A3 * B, B)).reshape(A3, B, B)
    return grad_values, grad_first, grad_second


def solution(mesh):
    return jax.shard_map(
        shards,
        mesh=mesh,
        in_specs=(
            P("dp", "seq", None),
            P("dp", "seq", None),
            P("dp", "seq", None),
            P("seq", None, None),
            P("seq", None, None),
        ),
        out_specs=(P("dp", "seq", None), P("seq", None, None), P("seq", None, None)),
        check_vma=False,
    )
```

```python
import jax
import jax.numpy as jnp
from jax import lax
from jax.experimental import pallas as pl
from jax.experimental.pallas import tpu as pltpu
from jax.sharding import PartitionSpec as P

X, Z, C, Y = 4, 8, 2, 4
F32, BF16 = jnp.float32, jnp.bfloat16
VMEM_BYTES = 56 * 2**20


def spot(x, z, c):
    return ((x % X) * Z + z % Z) * C + c % C


def moved(dx, dz, dc):
    return [
        (spot(x, z, c), spot(x + dx, z + dz, c + dc))
        for x in range(X)
        for z in range(Z)
        for c in range(C)
    ]


CHIPS = [[spot(x, z, c) for x in range(X) for z in range(Z)] for c in range(C)]


def hop(array, dx=0, dz=0, dc=0):
    return lax.ppermute(array, "seq", moved(dx, dz, dc))


def everywhere(array):
    return lax.all_to_all(array, "seq", 0, 0, axis_index_groups=CHIPS, tiled=True)


def params():
    return pltpu.CompilerParams(vmem_limit_bytes=VMEM_BYTES)


def cost(flops, moved_bytes):
    return pl.CostEstimate(flops=flops, bytes_accessed=moved_bytes, transcendentals=0)


def gate_kernel(gates_ref, grad_ref, out_ref):
    width = gates_ref.shape[-1]
    for n in range(gates_ref.shape[0]):
        p = gates_ref[n, 0].astype(F32) * grad_ref[n, 0].astype(F32)
        out_ref[:, :, 0, :, n * width : (n + 1) * width] = p.astype(BF16)


def gate(gates, grad_out):
    count, A3, _, _, C8, width = gates.shape
    spec = pl.BlockSpec((count, 1, X, Z, C8, width), lambda a: (0, a, 0, 0, 0, 0))
    return pl.pallas_call(
        gate_kernel,
        grid=(A3,),
        in_specs=[spec, spec],
        out_specs=pl.BlockSpec((X, Z, 1, C8, count * width), lambda a: (0, 0, a, 0, 0)),
        out_shape=jax.ShapeDtypeStruct((X, Z, A3, C8, count * width), BF16),
        compiler_params=params(),
        cost_estimate=cost(gates.size, 6 * gates.size),
        name="gate",
    )(gates, grad_out)


def mix_kernel(weights_ref, inputs_ref, out_ref):
    width = inputs_ref.shape[-1]
    for n in range(inputs_ref.shape[0]):
        mixed = jnp.dot(weights_ref[0], inputs_ref[n, 0], preferred_element_type=F32)
        mixed = mixed.astype(BF16).reshape(X, Z, -1, width)
        out_ref[:, :, 0, :, n * width : (n + 1) * width] = mixed


def mix(weights, inputs):
    count, A3, B, width = inputs.shape
    C8 = B // (X * Z)
    return pl.pallas_call(
        mix_kernel,
        grid=(A3,),
        in_specs=[
            pl.BlockSpec((1, B, B), lambda a: (a, 0, 0)),
            pl.BlockSpec((count, 1, B, width), lambda a: (0, a, 0, 0)),
        ],
        out_specs=pl.BlockSpec((X, Z, 1, C8, count * width), lambda a: (0, 0, a, 0, 0)),
        out_shape=jax.ShapeDtypeStruct((X, Z, A3, C8, count * width), BF16),
        compiler_params=params(),
        cost_estimate=cost(2 * inputs.size * B, 4 * inputs.size),
        name="mix",
    )(weights, inputs)


def inner_kernel(own_m_ref, other_m_ref, own_ref, other_ref, out_ref):
    total = jnp.dot(own_m_ref[...], own_ref[...], preferred_element_type=F32)
    total += jnp.dot(other_m_ref[...], other_ref[...], preferred_element_type=F32)
    out_ref[...] = total.astype(BF16)


def inner_product(own_m, other_m, own, other):
    rows, width = own.shape
    tile = 256
    whole = pl.BlockSpec((rows, rows), lambda i: (0, 0))
    part = pl.BlockSpec((rows, tile), lambda i: (0, i))
    return pl.pallas_call(
        inner_kernel,
        grid=(width // tile,),
        in_specs=[whole, whole, part, part],
        out_specs=part,
        out_shape=jax.ShapeDtypeStruct((rows, width), BF16),
        compiler_params=params(),
        cost_estimate=cost(4 * rows * rows * width, 6 * rows * width),
        name="inner",
    )(own_m, other_m, own, other)


def first_kernel(y_ref, inputs_ref, inner_ref, own_ref, *refs):
    outs, held = refs[: Y - 1], refs[Y - 1]
    y = y_ref[0]
    rows, width = inputs_ref.shape[2:]
    total = None
    for n in range(inputs_ref.shape[0]):
        inner = inner_ref[:, 0, :, n * width : (n + 1) * width].reshape(rows, width)
        product = lax.dot_general(
            inputs_ref[n, 0], inner, (((1,), (1,)), ((), ())), preferred_element_type=F32
        )
        total = product if total is None else total + product
    held[...] = total.reshape(held.shape)
    own_ref[0] = held[y]
    for k, out in enumerate(outs):
        out[0] = held[lax.rem(y + k + 1, Y)].astype(BF16)


def first_gradient(y, inputs, inner):
    count, A3, B, width = inputs.shape
    rows = B // Y
    index = lambda a, y: (a, 0, 0)
    part = (A3, rows, B)
    return pl.pallas_call(
        first_kernel,
        grid_spec=pltpu.PrefetchScalarGridSpec(
            num_scalar_prefetch=1,
            grid=(A3,),
            in_specs=[
                pl.BlockSpec((count, 1, B, width), lambda a, y: (0, a, 0, 0)),
                pl.BlockSpec((X * Z, 1, B // (X * Z), count * width), lambda a, y: (0, a, 0, 0)),
            ],
            out_specs=[pl.BlockSpec((1, rows, B), index)] * Y,
            scratch_shapes=[pltpu.VMEM((Y, rows, B), F32)],
        ),
        out_shape=[jax.ShapeDtypeStruct(part, F32)] + [jax.ShapeDtypeStruct(part, BF16)] * (Y - 1),
        compiler_params=params(),
        cost_estimate=cost(2 * inputs.size * B, 4 * inputs.size),
        name="first",
    )(y, inputs, inner)


def result_kernel(weights_ref, inner_ref, out_ref):
    rows, width = out_ref.shape[2:]
    for n in range(out_ref.shape[0]):
        inner = inner_ref[:, 0, :, n * width : (n + 1) * width].reshape(rows, width)
        product = jnp.dot(weights_ref[0], inner, preferred_element_type=F32)
        out_ref[n, 0] = product.astype(BF16)


def result(weights, inner, shape):
    count, A3, B, width = shape
    return pl.pallas_call(
        result_kernel,
        grid=(A3,),
        in_specs=[
            pl.BlockSpec((1, B, B), lambda a: (a, 0, 0)),
            pl.BlockSpec((X * Z, 1, B // (X * Z), count * width), lambda a: (0, a, 0, 0)),
        ],
        out_specs=pl.BlockSpec((count, 1, B, width), lambda a: (0, a, 0, 0)),
        out_shape=jax.ShapeDtypeStruct(shape, BF16),
        compiler_params=params(),
        cost_estimate=cost(2 * inner.size * B, 4 * inner.size),
        name="result",
    )(weights, inner)


def dp_hop(array, k):
    return lax.ppermute(array, "dp", [(i, (i + k) % Y) for i in range(Y)])


def place_kernel(y_ref, *refs):
    parts, out = refs[:Y], refs[Y]
    y = y_ref[0]
    rows = parts[0].shape[1]
    for k in range(Y):
        at = pl.multiple_of(lax.rem(y + Y - k, Y) * rows, rows)
        out[:, pl.ds(at, rows), :] = parts[k][...].astype(F32)


def dp_sum(y, own, sent):
    got = [dp_hop(piece, k + 1) for k, piece in enumerate(sent)]
    for piece in got:
        own = own + piece.astype(F32)
    small = own.astype(BF16)
    parts = [own] + [dp_hop(small, k) for k in range(1, Y)]
    scalar = pl.BlockSpec(memory_space=pltpu.SMEM)
    whole = pl.BlockSpec(memory_space=pltpu.VMEM)
    a, b, c = own.shape
    return pl.pallas_call(
        place_kernel,
        in_specs=[scalar] + [whole] * Y,
        out_specs=whole,
        out_shape=jax.ShapeDtypeStruct((a, b * Y, c), F32),
        compiler_params=params(),
        cost_estimate=cost(own.size, 6 * own.size),
        name="place",
    )(y, *parts)


def shards(values, gates, grad_out, first_blocks, second_blocks):
    count, rows, width = values.shape
    A3, B = first_blocks.shape[:2]
    C8 = B // (X * Z)
    C4, A = second_blocks.shape[:2]
    half = A // C
    tall = half * C8
    lanes = count * width
    here = lax.axis_index("seq").astype(jnp.int32)
    core = here % C
    ys = lax.axis_index("dp").astype(jnp.int32).reshape(1)

    gates = gates.reshape(count, A3, X, Z, C8, width)
    grad_out = grad_out.reshape(count, A3, X, Z, C8, width)
    gated = gate(gates, grad_out)
    own = everywhere(gated.reshape(X * Z, A3 * C8, lanes)).reshape(tall, lanes)

    values, first_blocks, second_blocks, _ = lax.optimization_barrier(
        (values, first_blocks, second_blocks, gated)
    )
    inputs = values.reshape(count, A3, B, width)
    mixed = mix(first_blocks.transpose(0, 2, 1), inputs)
    mixed, _ = lax.optimization_barrier((mixed, own))
    cols_u = everywhere(mixed.reshape(X * Z, A3 * C8, lanes)).reshape(tall, lanes)

    second = second_blocks.reshape(C4, half // A3, C, A3, A)
    mine = lax.dynamic_index_in_dim(second, core, 2, keepdims=False)
    other = hop(lax.dynamic_index_in_dim(second, 1 - core, 2, keepdims=False), dc=1)
    pair = jnp.where(core == 0, jnp.stack([mine, other]), jnp.stack([other, mine]))
    pair = pair.reshape(C8, half, A).transpose(1, 0, 2).reshape(tall, A)
    e = lax.broadcasted_iota(jnp.int32, (A, tall), 0)
    q = lax.broadcasted_iota(jnp.int32, (A, tall), 1) // C8
    spread = [
        (e == (q // A3) * (C * A3) + ((core + r) % C) * A3 + q % A3).astype(BF16) for r in range(C)
    ]
    same = (
        lax.broadcasted_iota(jnp.int32, (tall, tall), 0) % C8
        == lax.broadcasted_iota(jnp.int32, (tall, tall), 1) % C8
    )
    wide = [
        jnp.where(same, jnp.dot(pair, s, preferred_element_type=F32), 0).astype(BF16)
        for s in spread
    ]

    cols_g = (own, hop(own, dc=1))
    inner = inner_product(*wide, *cols_g)
    inner, _ = lax.optimization_barrier((inner, cols_u))
    inner = everywhere(inner.reshape(X * Z, A3 * C8, lanes)).reshape(X * Z, A3, C8, lanes)

    grad_second = 0
    for r in range(C):
        product = lax.dot_general(
            cols_u, cols_g[r], (((1,), (1,)), ((), ())), preferred_element_type=F32
        )
        grad_second += lax.dot_general(
            jnp.where(same, product, 0),
            spread[r].astype(F32),
            (((1,), (1,)), ((), ())),
            precision=lax.Precision.HIGHEST,
            preferred_element_type=F32,
        )
    grad_second = grad_second.reshape(half, C, C4, A).transpose(1, 2, 0, 3)
    mine = lax.dynamic_index_in_dim(grad_second, core, 0, keepdims=False)
    other = hop(lax.dynamic_index_in_dim(grad_second, 1 - core, 0, keepdims=False), dc=1)
    mine, other = (g.reshape(C4, half // A3, 1, A3, A) for g in (mine, other))
    pair = jnp.where(
        core == 0, jnp.concatenate([mine, other], 2), jnp.concatenate([other, mine], 2)
    )
    pair = pair.reshape(C4, A, A)
    parts = [
        lax.dynamic_slice_in_dim(pair, (ys[0] + k) % Y * (A // Y), A // Y, 1) for k in range(Y)
    ]
    grad_second = dp_sum(ys, parts[0], [part.astype(BF16) for part in parts[1:]])

    inner, grad_second = lax.optimization_barrier((inner, grad_second))

    own, *sent = first_gradient(ys, inputs, inner)
    grad_values = result(first_blocks, inner, inputs.shape).reshape(count, rows, width)
    own, grad_values = lax.optimization_barrier((own, grad_values))
    grad_first = dp_sum(ys, own, sent)
    return grad_values, grad_first, grad_second


def solution(mesh):
    return jax.shard_map(
        shards,
        mesh=mesh,
        in_specs=(
            P("dp", "seq", None),
            P("dp", "seq", None),
            P("dp", "seq", None),
            P("seq", None, None),
            P("seq", None, None),
        ),
        out_specs=(P("dp", "seq", None), P("seq", None, None), P("seq", None, None)),
        check_vma=False,
    )
```

```python
import jax
import jax.numpy as jnp
from jax import lax
from jax.experimental import pallas as pl
from jax.experimental.pallas import tpu as pltpu
from jax.sharding import PartitionSpec as P

X, Z, C, Y = 4, 8, 2, 4
F32, BF16 = jnp.float32, jnp.bfloat16
VMEM_BYTES = 62 * 2**20


def spot(x, z, c):
    return ((x % X) * Z + z % Z) * C + c % C


def moved(dx, dz, dc):
    return [
        (spot(x, z, c), spot(x + dx, z + dz, c + dc))
        for x in range(X)
        for z in range(Z)
        for c in range(C)
    ]


CHIPS = [[spot(x, z, c) for x in range(X) for z in range(Z)] for c in range(C)]


def hop(array, dx=0, dz=0, dc=0):
    return lax.ppermute(array, "seq", moved(dx, dz, dc))


def everywhere(array):
    return lax.all_to_all(array, "seq", 0, 0, axis_index_groups=CHIPS, tiled=True)


def params():
    return pltpu.CompilerParams(vmem_limit_bytes=VMEM_BYTES)


def cost(flops, moved_bytes):
    return pl.CostEstimate(flops=flops, bytes_accessed=moved_bytes, transcendentals=0)


def gate_kernel(gates, grad_out, out, gates_held, grad_held, out_held, in_sems, out_sems):
    count, A3 = gates.shape[:2]
    width = gates.shape[-1]
    reads, writes = [], []
    for a in range(A3):
        for n in range(count):
            pair = [
                pltpu.make_async_copy(gates.at[n, a], gates_held.at[n, a], in_sems.at[a, n, 0]),
                pltpu.make_async_copy(grad_out.at[n, a], grad_held.at[n, a], in_sems.at[a, n, 1]),
            ]
            for copy in pair:
                copy.start()
            reads.append(pair)
    for a in range(A3):
        for n in range(count):
            for copy in reads[a * count + n]:
                copy.wait()
            p = gates_held[n, a].astype(F32) * grad_held[n, a].astype(F32)
            out_held[:, :, a, :, n * width : (n + 1) * width] = p.astype(BF16)
        writes.append(pltpu.make_async_copy(out_held.at[:, :, a], out.at[:, :, a], out_sems.at[a]))
        writes[-1].start()
    for copy in writes:
        copy.wait()


def gate(gates, grad_out):
    count, A3, _, _, C8, width = gates.shape
    shape = (X, Z, A3, C8, count * width)
    anywhere = pl.BlockSpec(memory_space=pl.ANY)
    return pl.pallas_call(
        gate_kernel,
        in_specs=[anywhere] * 2,
        out_specs=anywhere,
        out_shape=jax.ShapeDtypeStruct(shape, BF16),
        scratch_shapes=[
            pltpu.VMEM(gates.shape, BF16),
            pltpu.VMEM(gates.shape, BF16),
            pltpu.VMEM(shape, BF16),
            pltpu.SemaphoreType.DMA((A3, count, 2)),
            pltpu.SemaphoreType.DMA((A3,)),
        ],
        compiler_params=params(),
        cost_estimate=cost(gates.size, 6 * gates.size),
        name="gate",
    )(gates, grad_out)


def mix_kernel(weights_ref, inputs_ref, out_ref):
    width = inputs_ref.shape[-1]
    for n in range(inputs_ref.shape[0]):
        mixed = jnp.dot(weights_ref[0], inputs_ref[n, 0], preferred_element_type=F32)
        mixed = mixed.astype(BF16).reshape(X, Z, -1, width)
        out_ref[:, :, 0, :, n * width : (n + 1) * width] = mixed


def mix(weights, inputs):
    count, A3, B, width = inputs.shape
    C8 = B // (X * Z)
    return pl.pallas_call(
        mix_kernel,
        grid=(A3,),
        in_specs=[
            pl.BlockSpec((1, B, B), lambda a: (a, 0, 0)),
            pl.BlockSpec((count, 1, B, width), lambda a: (0, a, 0, 0)),
        ],
        out_specs=pl.BlockSpec((X, Z, 1, C8, count * width), lambda a: (0, 0, a, 0, 0)),
        out_shape=jax.ShapeDtypeStruct((X, Z, A3, C8, count * width), BF16),
        compiler_params=params(),
        cost_estimate=cost(2 * inputs.size * B, 4 * inputs.size),
        name="mix",
    )(weights, inputs)


def inner_kernel(own_m_ref, other_m_ref, own_ref, other_ref, out_ref):
    total = jnp.dot(own_m_ref[...], own_ref[...], preferred_element_type=F32)
    total += jnp.dot(other_m_ref[...], other_ref[...], preferred_element_type=F32)
    out_ref[...] = total.astype(BF16)


def inner_product(own_m, other_m, own, other):
    rows, width = own.shape
    tile = 512
    whole = pl.BlockSpec((rows, rows), lambda i: (0, 0))
    part = pl.BlockSpec((rows, tile), lambda i: (0, i))
    return pl.pallas_call(
        inner_kernel,
        grid=(width // tile,),
        in_specs=[whole, whole, part, part],
        out_specs=part,
        out_shape=jax.ShapeDtypeStruct((rows, width), BF16),
        compiler_params=params(),
        cost_estimate=cost(4 * rows * rows * width, 6 * rows * width),
        name="inner",
    )(own_m, other_m, own, other)


def first_kernel(inputs_ref, inner_ref, own_ref, sent_ref):
    rows, width = inputs_ref.shape[2:]
    total = None
    for n in range(inputs_ref.shape[0]):
        inner = inner_ref[:, 0, :, n * width : (n + 1) * width].reshape(rows, width)
        product = lax.dot_general(
            inputs_ref[n, 0], inner, (((1,), (1,)), ((), ())), preferred_element_type=F32
        )
        total = product if total is None else total + product
    own_ref[0] = total
    sent_ref[0] = total.astype(BF16)


def first_gradient(inputs, inner):
    count, A3, B, width = inputs.shape
    index = lambda a: (a, 0, 0)
    shape = (A3, B, B)
    return pl.pallas_call(
        first_kernel,
        grid=(A3,),
        in_specs=[
            pl.BlockSpec((count, 1, B, width), lambda a: (0, a, 0, 0)),
            pl.BlockSpec((X * Z, 1, B // (X * Z), count * width), lambda a: (0, a, 0, 0)),
        ],
        out_specs=[pl.BlockSpec((1, B, B), index)] * 2,
        out_shape=[jax.ShapeDtypeStruct(shape, F32), jax.ShapeDtypeStruct(shape, BF16)],
        compiler_params=params(),
        cost_estimate=cost(2 * inputs.size * B, 4 * inputs.size),
        name="first",
    )(inputs, inner)


def result_kernel(weights_ref, inner_ref, out_ref):
    rows, width = out_ref.shape[2:]
    for n in range(out_ref.shape[0]):
        inner = inner_ref[:, 0, :, n * width : (n + 1) * width].reshape(rows, width)
        product = jnp.dot(weights_ref[0], inner, preferred_element_type=F32)
        out_ref[n, 0] = product.astype(BF16)


def result(weights, inner, shape):
    count, A3, B, width = shape
    return pl.pallas_call(
        result_kernel,
        grid=(A3,),
        in_specs=[
            pl.BlockSpec((1, B, B), lambda a: (a, 0, 0)),
            pl.BlockSpec((X * Z, 1, B // (X * Z), count * width), lambda a: (0, a, 0, 0)),
        ],
        out_specs=pl.BlockSpec((count, 1, B, width), lambda a: (0, a, 0, 0)),
        out_shape=jax.ShapeDtypeStruct(shape, BF16),
        compiler_params=params(),
        cost_estimate=cost(2 * inner.size * B, 4 * inner.size),
        name="result",
    )(weights, inner)


def dp_hop(array, k):
    return lax.ppermute(array, "dp", [(i, (i + k) % Y) for i in range(Y)])


def dp_sum(own, sent):
    for k in range(1, Y):
        own = own + dp_hop(sent, k).astype(F32)
    return own


def shards(values, gates, grad_out, first_blocks, second_blocks):
    count, rows, width = values.shape
    A3, B = first_blocks.shape[:2]
    C8 = B // (X * Z)
    C4, A = second_blocks.shape[:2]
    half = A // C
    tall = half * C8
    lanes = count * width
    here = lax.axis_index("seq").astype(jnp.int32)
    core = here % C

    gates = gates.reshape(count, A3, X, Z, C8, width)
    grad_out = grad_out.reshape(count, A3, X, Z, C8, width)
    gated = gate(gates, grad_out)
    own = everywhere(gated.reshape(X * Z, A3 * C8, lanes)).reshape(tall, lanes)

    values, first_blocks, second_blocks, _ = lax.optimization_barrier(
        (values, first_blocks, second_blocks, gated)
    )
    inputs = values.reshape(count, A3, B, width)
    mixed = mix(first_blocks.transpose(0, 2, 1), inputs)
    mixed, _ = lax.optimization_barrier((mixed, own))
    cols_u = everywhere(mixed.reshape(X * Z, A3 * C8, lanes)).reshape(tall, lanes)

    second = second_blocks.reshape(C4, half // A3, C, A3, A)
    mine = lax.dynamic_index_in_dim(second, core, 2, keepdims=False)
    other = hop(lax.dynamic_index_in_dim(second, 1 - core, 2, keepdims=False), dc=1)
    pair = jnp.where(core == 0, jnp.stack([mine, other]), jnp.stack([other, mine]))
    pair = pair.reshape(C8, half, A).transpose(1, 0, 2).reshape(tall, A)
    e = lax.broadcasted_iota(jnp.int32, (A, tall), 0)
    q = lax.broadcasted_iota(jnp.int32, (A, tall), 1) // C8
    spread = [
        (e == (q // A3) * (C * A3) + ((core + r) % C) * A3 + q % A3).astype(BF16) for r in range(C)
    ]
    same = (
        lax.broadcasted_iota(jnp.int32, (tall, tall), 0) % C8
        == lax.broadcasted_iota(jnp.int32, (tall, tall), 1) % C8
    )
    wide = [
        jnp.where(same, jnp.dot(pair, s, preferred_element_type=F32), 0).astype(BF16)
        for s in spread
    ]

    cols_g = (own, hop(own, dc=1))
    inner = inner_product(*wide, *cols_g)
    inner, _ = lax.optimization_barrier((inner, cols_u))
    inner = everywhere(inner.reshape(X * Z, A3 * C8, lanes)).reshape(X * Z, A3, C8, lanes)

    grad_second = 0
    for r in range(C):
        product = lax.dot_general(
            cols_u, cols_g[r], (((1,), (1,)), ((), ())), preferred_element_type=F32
        )
        grad_second += lax.dot_general(
            jnp.where(same, product, 0),
            spread[r].astype(F32),
            (((1,), (1,)), ((), ())),
            precision=lax.Precision.HIGHEST,
            preferred_element_type=F32,
        )
    grad_second = grad_second.reshape(half, C, C4, A).transpose(1, 2, 0, 3)
    mine = lax.dynamic_index_in_dim(grad_second, core, 0, keepdims=False)
    other = hop(lax.dynamic_index_in_dim(grad_second, 1 - core, 0, keepdims=False), dc=1)
    mine, other = (g.reshape(C4, half // A3, 1, A3, A) for g in (mine, other))
    pair = jnp.where(
        core == 0, jnp.concatenate([mine, other], 2), jnp.concatenate([other, mine], 2)
    )
    pair = pair.reshape(C4, A, A)
    grad_second = dp_sum(pair, pair.astype(BF16))
    inner, grad_second = lax.optimization_barrier((inner, grad_second))

    own, sent = first_gradient(inputs, inner)
    grad_values = result(first_blocks, inner, inputs.shape).reshape(count, rows, width)
    own, grad_values = lax.optimization_barrier((own, grad_values))
    return grad_values, dp_sum(own, sent), grad_second


def solution(mesh):
    return jax.shard_map(
        shards,
        mesh=mesh,
        in_specs=(
            P("dp", "seq", None),
            P("dp", "seq", None),
            P("dp", "seq", None),
            P("seq", None, None),
            P("seq", None, None),
        ),
        out_specs=(P("dp", "seq", None), P("seq", None, None), P("seq", None, None)),
        check_vma=False,
    )
```

```python
import jax
import jax.numpy as jnp
from jax import lax
from jax.experimental import pallas as pl
from jax.experimental.pallas import tpu as pltpu
from jax.sharding import PartitionSpec as P

X, Z, C, Y = 4, 8, 2, 4
F32, BF16 = jnp.float32, jnp.bfloat16
VMEM_BYTES = 62 * 2**20


def spot(x, z, c):
    return ((x % X) * Z + z % Z) * C + c % C


def moved(dx, dz, dc):
    return [
        (spot(x, z, c), spot(x + dx, z + dz, c + dc))
        for x in range(X)
        for z in range(Z)
        for c in range(C)
    ]


CHIPS = [[spot(x, z, c) for x in range(X) for z in range(Z)] for c in range(C)]


def hop(array, dx=0, dz=0, dc=0):
    return lax.ppermute(array, "seq", moved(dx, dz, dc))


def everywhere(array):
    return lax.all_to_all(array, "seq", 0, 0, axis_index_groups=CHIPS, tiled=True)


def params():
    return pltpu.CompilerParams(vmem_limit_bytes=VMEM_BYTES)


def cost(flops, moved_bytes):
    return pl.CostEstimate(flops=flops, bytes_accessed=moved_bytes, transcendentals=0)


def gate_kernel(gates, grad_out, out, gates_held, grad_held, out_held, in_sems, out_sems):
    count, A3 = gates.shape[:2]
    width = gates.shape[-1]
    reads, writes = [], []
    for a in range(A3):
        for n in range(count):
            pair = [
                pltpu.make_async_copy(gates.at[n, a], gates_held.at[n, a], in_sems.at[a, n, 0]),
                pltpu.make_async_copy(grad_out.at[n, a], grad_held.at[n, a], in_sems.at[a, n, 1]),
            ]
            for copy in pair:
                copy.start()
            reads.append(pair)
    for a in range(A3):
        for n in range(count):
            for copy in reads[a * count + n]:
                copy.wait()
            p = gates_held[n, a].astype(F32) * grad_held[n, a].astype(F32)
            out_held[:, :, a, :, n * width : (n + 1) * width] = p.astype(BF16)
        writes.append(pltpu.make_async_copy(out_held.at[:, :, a], out.at[:, :, a], out_sems.at[a]))
        writes[-1].start()
    for copy in writes:
        copy.wait()


def gate(gates, grad_out):
    count, A3, _, _, C8, width = gates.shape
    shape = (X, Z, A3, C8, count * width)
    anywhere = pl.BlockSpec(memory_space=pl.ANY)
    return pl.pallas_call(
        gate_kernel,
        in_specs=[anywhere] * 2,
        out_specs=anywhere,
        out_shape=jax.ShapeDtypeStruct(shape, BF16),
        scratch_shapes=[
            pltpu.VMEM(gates.shape, BF16),
            pltpu.VMEM(gates.shape, BF16),
            pltpu.VMEM(shape, BF16),
            pltpu.SemaphoreType.DMA((A3, count, 2)),
            pltpu.SemaphoreType.DMA((A3,)),
        ],
        compiler_params=params(),
        cost_estimate=cost(gates.size, 6 * gates.size),
        name="gate",
    )(gates, grad_out)


def mix_kernel(weights_ref, inputs_ref, out_ref):
    width = inputs_ref.shape[-1]
    for n in range(inputs_ref.shape[0]):
        mixed = jnp.dot(weights_ref[0], inputs_ref[n, 0], preferred_element_type=F32)
        mixed = mixed.astype(BF16).reshape(X, Z, -1, width)
        out_ref[:, :, 0, :, n * width : (n + 1) * width] = mixed


def mix(weights, inputs):
    count, A3, B, width = inputs.shape
    C8 = B // (X * Z)
    return pl.pallas_call(
        mix_kernel,
        grid=(A3,),
        in_specs=[
            pl.BlockSpec((1, B, B), lambda a: (a, 0, 0)),
            pl.BlockSpec((count, 1, B, width), lambda a: (0, a, 0, 0)),
        ],
        out_specs=pl.BlockSpec((X, Z, 1, C8, count * width), lambda a: (0, 0, a, 0, 0)),
        out_shape=jax.ShapeDtypeStruct((X, Z, A3, C8, count * width), BF16),
        compiler_params=params(),
        cost_estimate=cost(2 * inputs.size * B, 4 * inputs.size),
        name="mix",
    )(weights, inputs)


def inner_kernel(own_m_ref, other_m_ref, own_ref, other_ref, out_ref):
    total = jnp.dot(own_m_ref[...], own_ref[...], preferred_element_type=F32)
    total += jnp.dot(other_m_ref[...], other_ref[...], preferred_element_type=F32)
    out_ref[...] = total.astype(BF16)


def inner_product(own_m, other_m, own, other):
    rows, width = own.shape
    tile = 512
    whole = pl.BlockSpec((rows, rows), lambda i: (0, 0))
    part = pl.BlockSpec((rows, tile), lambda i: (0, i))
    return pl.pallas_call(
        inner_kernel,
        grid=(width // tile,),
        in_specs=[whole, whole, part, part],
        out_specs=part,
        out_shape=jax.ShapeDtypeStruct((rows, width), BF16),
        compiler_params=params(),
        cost_estimate=cost(4 * rows * rows * width, 6 * rows * width),
        name="inner",
    )(own_m, other_m, own, other)


def first_kernel(inputs_ref, inner_ref, own_ref, sent_ref):
    rows, width = inputs_ref.shape[2:]
    total = None
    for n in range(inputs_ref.shape[0]):
        inner = inner_ref[:, 0, :, n * width : (n + 1) * width].reshape(rows, width)
        product = lax.dot_general(
            inputs_ref[n, 0], inner, (((1,), (1,)), ((), ())), preferred_element_type=F32
        )
        total = product if total is None else total + product
    own_ref[0] = total
    sent_ref[0] = total.astype(BF16)


def first_gradient(inputs, inner):
    count, A3, B, width = inputs.shape
    index = lambda a: (a, 0, 0)
    shape = (A3, B, B)
    return pl.pallas_call(
        first_kernel,
        grid=(A3,),
        in_specs=[
            pl.BlockSpec((count, 1, B, width), lambda a: (0, a, 0, 0)),
            pl.BlockSpec((X * Z, 1, B // (X * Z), count * width), lambda a: (0, a, 0, 0)),
        ],
        out_specs=[pl.BlockSpec((1, B, B), index)] * 2,
        out_shape=[jax.ShapeDtypeStruct(shape, F32), jax.ShapeDtypeStruct(shape, BF16)],
        compiler_params=params(),
        cost_estimate=cost(2 * inputs.size * B, 4 * inputs.size),
        name="first",
    )(inputs, inner)


def result_kernel(weights_ref, inner_ref, out_ref):
    rows, width = out_ref.shape[2:]
    for n in range(out_ref.shape[0]):
        inner = inner_ref[:, 0, :, n * width : (n + 1) * width].reshape(rows, width)
        product = jnp.dot(weights_ref[0], inner, preferred_element_type=F32)
        out_ref[n, 0] = product.astype(BF16)


def result(weights, inner, shape):
    count, A3, B, width = shape
    return pl.pallas_call(
        result_kernel,
        grid=(A3,),
        in_specs=[
            pl.BlockSpec((1, B, B), lambda a: (a, 0, 0)),
            pl.BlockSpec((X * Z, 1, B // (X * Z), count * width), lambda a: (0, a, 0, 0)),
        ],
        out_specs=pl.BlockSpec((count, 1, B, width), lambda a: (0, a, 0, 0)),
        out_shape=jax.ShapeDtypeStruct(shape, BF16),
        compiler_params=params(),
        cost_estimate=cost(2 * inner.size * B, 4 * inner.size),
        name="result",
    )(weights, inner)


def dp_hop(array, k):
    return lax.ppermute(array, "dp", [(i, (i + k) % Y) for i in range(Y)])


def dp_sum(own, sent):
    for k in range(1, Y):
        own = own + dp_hop(sent, k).astype(F32)
    return own


def shards(values, gates, grad_out, first_blocks, second_blocks):
    count, rows, width = values.shape
    A3, B = first_blocks.shape[:2]
    C8 = B // (X * Z)
    C4, A = second_blocks.shape[:2]
    half = A // C
    tall = half * C8
    lanes = count * width
    here = lax.axis_index("seq").astype(jnp.int32)
    core = here % C

    gates = gates.reshape(count, A3, X, Z, C8, width)
    grad_out = grad_out.reshape(count, A3, X, Z, C8, width)
    gated = gate(gates, grad_out)
    own = everywhere(gated.reshape(X * Z, A3 * C8, lanes)).reshape(tall, lanes)

    values, first_blocks, second_blocks, _ = lax.optimization_barrier(
        (values, first_blocks, second_blocks, gated)
    )
    inputs = values.reshape(count, A3, B, width)
    mixed = mix(first_blocks.transpose(0, 2, 1), inputs)
    mixed, _ = lax.optimization_barrier((mixed, own))
    cols_u = everywhere(mixed.reshape(X * Z, A3 * C8, lanes)).reshape(tall, lanes)

    second = second_blocks.reshape(C4, half // A3, C, A3, A)
    mine = lax.dynamic_index_in_dim(second, core, 2, keepdims=False)
    other = hop(lax.dynamic_index_in_dim(second, 1 - core, 2, keepdims=False), dc=1)
    pair = jnp.where(core == 0, jnp.stack([mine, other]), jnp.stack([other, mine]))
    pair = pair.reshape(C8, half, A).transpose(1, 0, 2).reshape(tall, A)
    e = lax.broadcasted_iota(jnp.int32, (A, tall), 0)
    q = lax.broadcasted_iota(jnp.int32, (A, tall), 1) // C8
    spread = [
        (e == (q // A3) * (C * A3) + ((core + r) % C) * A3 + q % A3).astype(BF16) for r in range(C)
    ]
    same = (
        lax.broadcasted_iota(jnp.int32, (tall, tall), 0) % C8
        == lax.broadcasted_iota(jnp.int32, (tall, tall), 1) % C8
    )
    wide = [
        jnp.where(same, jnp.dot(pair, s, preferred_element_type=F32), 0).astype(BF16)
        for s in spread
    ]

    cols_g = (own, hop(own, dc=1))
    inner = inner_product(*wide, *cols_g)
    inner, _ = lax.optimization_barrier((inner, cols_u))
    inner = everywhere(inner.reshape(X * Z, A3 * C8, lanes)).reshape(X * Z, A3, C8, lanes)

    grad_second = 0
    for r in range(C):
        product = lax.dot_general(
            cols_u, cols_g[r], (((1,), (1,)), ((), ())), preferred_element_type=F32
        )
        grad_second += lax.dot_general(
            jnp.where(same, product, 0),
            spread[r].astype(F32),
            (((1,), (1,)), ((), ())),
            precision=lax.Precision.HIGHEST,
            preferred_element_type=F32,
        )
    grad_second = grad_second.reshape(half, C, C4, A).transpose(1, 2, 0, 3)
    mine = lax.dynamic_index_in_dim(grad_second, core, 0, keepdims=False)
    other = hop(lax.dynamic_index_in_dim(grad_second, 1 - core, 0, keepdims=False), dc=1)
    mine, other = (g.reshape(C4, half // A3, 1, A3, A) for g in (mine, other))
    pair = jnp.where(
        core == 0, jnp.concatenate([mine, other], 2), jnp.concatenate([other, mine], 2)
    )
    pair = pair.reshape(C4, A, A)
    grad_second = dp_sum(pair, pair.astype(BF16))
    inner, grad_second = lax.optimization_barrier((inner, grad_second))

    own, sent = first_gradient(inputs, inner)
    got = [dp_hop(sent, k) for k in range(1, Y)]
    grad_values = result(first_blocks, inner, inputs.shape).reshape(count, rows, width)
    got, grad_values = lax.optimization_barrier((got, grad_values))
    for piece in got:
        own = own + piece.astype(F32)
    return grad_values, own, grad_second


def solution(mesh):
    return jax.shard_map(
        shards,
        mesh=mesh,
        in_specs=(
            P("dp", "seq", None),
            P("dp", "seq", None),
            P("dp", "seq", None),
            P("seq", None, None),
            P("seq", None, None),
        ),
        out_specs=(P("dp", "seq", None), P("seq", None, None), P("seq", None, None)),
        check_vma=False,
    )
```

```python
import jax
import jax.numpy as jnp
from jax import lax
from jax.experimental import pallas as pl
from jax.experimental.pallas import tpu as pltpu
from jax.sharding import PartitionSpec as P

X, Z, C, Y = 4, 8, 2, 4
F32, BF16 = jnp.float32, jnp.bfloat16
VMEM_BYTES = 62 * 2**20


def spot(x, z, c):
    return ((x % X) * Z + z % Z) * C + c % C


def moved(dx, dz, dc):
    return [
        (spot(x, z, c), spot(x + dx, z + dz, c + dc))
        for x in range(X)
        for z in range(Z)
        for c in range(C)
    ]


CHIPS = [[spot(x, z, c) for x in range(X) for z in range(Z)] for c in range(C)]


def hop(array, dx=0, dz=0, dc=0):
    return lax.ppermute(array, "seq", moved(dx, dz, dc))


def everywhere(array):
    return lax.all_to_all(array, "seq", 0, 0, axis_index_groups=CHIPS, tiled=True)


def params():
    return pltpu.CompilerParams(vmem_limit_bytes=VMEM_BYTES)


def cost(flops, moved_bytes):
    return pl.CostEstimate(flops=flops, bytes_accessed=moved_bytes, transcendentals=0)


def gate_kernel(gates, grad_out, out, gates_held, grad_held, out_held, in_sems, out_sems):
    count, A3 = gates.shape[:2]
    width = gates.shape[-1]
    reads, writes = [], []
    for a in range(A3):
        for n in range(count):
            pair = [
                pltpu.make_async_copy(gates.at[n, a], gates_held.at[n, a], in_sems.at[a, n, 0]),
                pltpu.make_async_copy(grad_out.at[n, a], grad_held.at[n, a], in_sems.at[a, n, 1]),
            ]
            for copy in pair:
                copy.start()
            reads.append(pair)
    for a in range(A3):
        for n in range(count):
            for copy in reads[a * count + n]:
                copy.wait()
            p = gates_held[n, a].astype(F32) * grad_held[n, a].astype(F32)
            out_held[:, :, a, :, n * width : (n + 1) * width] = p.astype(BF16)
        writes.append(pltpu.make_async_copy(out_held.at[:, :, a], out.at[:, :, a], out_sems.at[a]))
        writes[-1].start()
    for copy in writes:
        copy.wait()


def gate(gates, grad_out):
    count, A3, _, _, C8, width = gates.shape
    shape = (X, Z, A3, C8, count * width)
    anywhere = pl.BlockSpec(memory_space=pl.ANY)
    return pl.pallas_call(
        gate_kernel,
        in_specs=[anywhere] * 2,
        out_specs=anywhere,
        out_shape=jax.ShapeDtypeStruct(shape, BF16),
        scratch_shapes=[
            pltpu.VMEM(gates.shape, BF16),
            pltpu.VMEM(gates.shape, BF16),
            pltpu.VMEM(shape, BF16),
            pltpu.SemaphoreType.DMA((A3, count, 2)),
            pltpu.SemaphoreType.DMA((A3,)),
        ],
        compiler_params=params(),
        cost_estimate=cost(gates.size, 6 * gates.size),
        name="gate",
    )(gates, grad_out)


def mix_kernel(weights_ref, inputs_ref, out_ref):
    width = inputs_ref.shape[-1]
    for n in range(inputs_ref.shape[0]):
        mixed = jnp.dot(weights_ref[0], inputs_ref[n, 0], preferred_element_type=F32)
        mixed = mixed.astype(BF16).reshape(X, Z, -1, width)
        out_ref[:, :, 0, :, n * width : (n + 1) * width] = mixed


def mix(weights, inputs):
    count, A3, B, width = inputs.shape
    C8 = B // (X * Z)
    return pl.pallas_call(
        mix_kernel,
        grid=(A3,),
        in_specs=[
            pl.BlockSpec((1, B, B), lambda a: (a, 0, 0)),
            pl.BlockSpec((count, 1, B, width), lambda a: (0, a, 0, 0)),
        ],
        out_specs=pl.BlockSpec((X, Z, 1, C8, count * width), lambda a: (0, 0, a, 0, 0)),
        out_shape=jax.ShapeDtypeStruct((X, Z, A3, C8, count * width), BF16),
        compiler_params=params(),
        cost_estimate=cost(2 * inputs.size * B, 4 * inputs.size),
        name="mix",
    )(weights, inputs)


def inner_kernel(own_m_ref, other_m_ref, own_ref, other_ref, out_ref):
    total = jnp.dot(own_m_ref[...], own_ref[...], preferred_element_type=F32)
    total += jnp.dot(other_m_ref[...], other_ref[...], preferred_element_type=F32)
    out_ref[...] = total.astype(BF16)


def inner_product(own_m, other_m, own, other):
    rows, width = own.shape
    tile = 512
    whole = pl.BlockSpec((rows, rows), lambda i: (0, 0))
    part = pl.BlockSpec((rows, tile), lambda i: (0, i))
    return pl.pallas_call(
        inner_kernel,
        grid=(width // tile,),
        in_specs=[whole, whole, part, part],
        out_specs=part,
        out_shape=jax.ShapeDtypeStruct((rows, width), BF16),
        compiler_params=params(),
        cost_estimate=cost(4 * rows * rows * width, 6 * rows * width),
        name="inner",
    )(own_m, other_m, own, other)


def first_kernel(inputs_ref, inner_ref, own_ref, left_ref, right_ref):
    rows, width = inputs_ref.shape[2:]
    total = None
    for n in range(inputs_ref.shape[0]):
        inner = inner_ref[:, 0, :, n * width : (n + 1) * width].reshape(rows, width)
        product = lax.dot_general(
            inputs_ref[n, 0], inner, (((1,), (1,)), ((), ())), preferred_element_type=F32
        )
        total = product if total is None else total + product
    own_ref[0] = total
    half = total.shape[1] // 2
    left_ref[0] = total[:, :half].astype(BF16)
    right_ref[0] = total[:, half:].astype(BF16)


def first_gradient(inputs, inner):
    count, A3, B, width = inputs.shape
    index = lambda a: (a, 0, 0)
    half = jax.ShapeDtypeStruct((A3, B, B // 2), BF16)
    return pl.pallas_call(
        first_kernel,
        grid=(A3,),
        in_specs=[
            pl.BlockSpec((count, 1, B, width), lambda a: (0, a, 0, 0)),
            pl.BlockSpec((X * Z, 1, B // (X * Z), count * width), lambda a: (0, a, 0, 0)),
        ],
        out_specs=[pl.BlockSpec((1, B, B), index)] + [pl.BlockSpec((1, B, B // 2), index)] * 2,
        out_shape=[jax.ShapeDtypeStruct((A3, B, B), F32), half, half],
        compiler_params=params(),
        cost_estimate=cost(2 * inputs.size * B, 4 * inputs.size),
        name="first",
    )(inputs, inner)


def result_kernel(weights_ref, inner_ref, out_ref):
    rows, width = out_ref.shape[2:]
    for n in range(out_ref.shape[0]):
        inner = inner_ref[:, 0, :, n * width : (n + 1) * width].reshape(rows, width)
        product = jnp.dot(weights_ref[0], inner, preferred_element_type=F32)
        out_ref[n, 0] = product.astype(BF16)


def result(weights, inner, shape):
    count, A3, B, width = shape
    return pl.pallas_call(
        result_kernel,
        grid=(A3,),
        in_specs=[
            pl.BlockSpec((1, B, B), lambda a: (a, 0, 0)),
            pl.BlockSpec((X * Z, 1, B // (X * Z), count * width), lambda a: (0, a, 0, 0)),
        ],
        out_specs=pl.BlockSpec((count, 1, B, width), lambda a: (0, a, 0, 0)),
        out_shape=jax.ShapeDtypeStruct(shape, BF16),
        compiler_params=params(),
        cost_estimate=cost(2 * inner.size * B, 4 * inner.size),
        name="result",
    )(weights, inner)


def dp_hop(array, k):
    return lax.ppermute(array, "dp", [(i, (i + k) % Y) for i in range(Y)])


def dp_sum(own, sent):
    for k in range(1, Y):
        own = own + dp_hop(sent, k).astype(F32)
    return own


def shards(values, gates, grad_out, first_blocks, second_blocks):
    count, rows, width = values.shape
    A3, B = first_blocks.shape[:2]
    C8 = B // (X * Z)
    C4, A = second_blocks.shape[:2]
    half = A // C
    tall = half * C8
    lanes = count * width
    here = lax.axis_index("seq").astype(jnp.int32)
    core = here % C

    gates = gates.reshape(count, A3, X, Z, C8, width)
    grad_out = grad_out.reshape(count, A3, X, Z, C8, width)
    gated = gate(gates, grad_out)
    own = everywhere(gated.reshape(X * Z, A3 * C8, lanes)).reshape(tall, lanes)

    values, first_blocks, second_blocks, _ = lax.optimization_barrier(
        (values, first_blocks, second_blocks, gated)
    )
    inputs = values.reshape(count, A3, B, width)
    mixed = mix(first_blocks.transpose(0, 2, 1), inputs)
    mixed, _ = lax.optimization_barrier((mixed, own))
    cols_u = everywhere(mixed.reshape(X * Z, A3 * C8, lanes)).reshape(tall, lanes)

    second = second_blocks.reshape(C4, half // A3, C, A3, A)
    mine = lax.dynamic_index_in_dim(second, core, 2, keepdims=False)
    other = hop(lax.dynamic_index_in_dim(second, 1 - core, 2, keepdims=False), dc=1)
    pair = jnp.where(core == 0, jnp.stack([mine, other]), jnp.stack([other, mine]))
    pair = pair.reshape(C8, half, A).transpose(1, 0, 2).reshape(tall, A)
    e = lax.broadcasted_iota(jnp.int32, (A, tall), 0)
    q = lax.broadcasted_iota(jnp.int32, (A, tall), 1) // C8
    spread = [
        (e == (q // A3) * (C * A3) + ((core + r) % C) * A3 + q % A3).astype(BF16) for r in range(C)
    ]
    same = (
        lax.broadcasted_iota(jnp.int32, (tall, tall), 0) % C8
        == lax.broadcasted_iota(jnp.int32, (tall, tall), 1) % C8
    )
    wide = [
        jnp.where(same, jnp.dot(pair, s, preferred_element_type=F32), 0).astype(BF16)
        for s in spread
    ]

    cols_g = (own, hop(own, dc=1))
    inner = inner_product(*wide, *cols_g)
    inner, _ = lax.optimization_barrier((inner, cols_u))
    inner = everywhere(inner.reshape(X * Z, A3 * C8, lanes)).reshape(X * Z, A3, C8, lanes)

    grad_second = 0
    for r in range(C):
        product = lax.dot_general(
            cols_u, cols_g[r], (((1,), (1,)), ((), ())), preferred_element_type=F32
        )
        grad_second += lax.dot_general(
            jnp.where(same, product, 0),
            spread[r].astype(F32),
            (((1,), (1,)), ((), ())),
            precision=lax.Precision.HIGHEST,
            preferred_element_type=F32,
        )
    grad_second = grad_second.reshape(half, C, C4, A).transpose(1, 2, 0, 3)
    mine = lax.dynamic_index_in_dim(grad_second, core, 0, keepdims=False)
    other = hop(lax.dynamic_index_in_dim(grad_second, 1 - core, 0, keepdims=False), dc=1)
    mine, other = (g.reshape(C4, half // A3, 1, A3, A) for g in (mine, other))
    pair = jnp.where(
        core == 0, jnp.concatenate([mine, other], 2), jnp.concatenate([other, mine], 2)
    )
    pair = pair.reshape(C4, A, A)
    grad_second = dp_sum(pair, pair.astype(BF16))
    inner, grad_second = lax.optimization_barrier((inner, grad_second))

    own, left, right = first_gradient(inputs, inner)
    left_below, right_above = dp_hop(left, 1), dp_hop(right, Y - 1)
    right_below, left_above = dp_hop(right, 1), dp_hop(left, Y - 1)
    halves = [
        (left_below, right_below),
        (left_above, right_above),
        (dp_hop(left_below, 1), dp_hop(right_above, Y - 1)),
    ]
    grad_values = result(first_blocks, inner, inputs.shape).reshape(count, rows, width)
    halves, grad_values = lax.optimization_barrier((halves, grad_values))
    got = [jnp.concatenate(pair, 2) for pair in halves]
    for piece in got:
        own = own + piece.astype(F32)
    return grad_values, own, grad_second


def solution(mesh):
    return jax.shard_map(
        shards,
        mesh=mesh,
        in_specs=(
            P("dp", "seq", None),
            P("dp", "seq", None),
            P("dp", "seq", None),
            P("seq", None, None),
            P("seq", None, None),
        ),
        out_specs=(P("dp", "seq", None), P("seq", None, None), P("seq", None, None)),
        check_vma=False,
    )
```
